512 devices in a mesh: blk: 64 (over x_lo, z, core), tp: 8 (over x_hi, y).
Axes of the slice: x: 4 (x_hi: 2, x_lo: 2; x = x_hi * 2 + x_lo), y: 4, z: 16, core: 2. Of those that a mesh axis runs over, the one named last changes fastest.
Arguments:
- tokens: bfloat16 [32768, 8192], P('blk', 'tp'), may hold values from -40 to 40
- gain: float32 [8192], P('tp'), may hold values from 0.1 to 1.9
- w_value: bfloat16 [8192, 1024], P(('tp', 'blk')), may hold values from -0.0625 to 0.0625
- cotangent: bfloat16 [32768, 1024], P('blk'), may hold values from -6 to 6
Outputs:
- values: bfloat16 [32768, 1024], P('blk')
- grad_weight: float32 [8192, 1024], P(('tp', 'blk'))
- grad_tokens: bfloat16 [32768, 8192], P('blk', 'tp')
The draws below stay inside these ranges and needn't reach their ends.
All inputs are finite; a program needn't handle non-finite values.
Results may differ from the reference program's by a relative error of at most 0.0049.
Values may be sent and summed in bfloat16 or wider, within the bound.
A program may use at most 64 MiB of HBM per device.

```python
import math
import jax
import jax.numpy as jnp
from jax import lax

D = 8192
KV = 1024
TOKENS = 32768


def draw_tokens(key, part):
    key = jax.random.fold_in(key, 11)
    kr, kc, kb = jax.random.split(key, 3)
    rows = jnp.exp(jax.random.uniform(kr, (TOKENS, 1), jnp.float32) * math.log(10.0))
    cols = jnp.exp(jax.random.uniform(kc, (1, D), jnp.float32) * math.log(3.0))
    base = jax.random.normal(kb, (TOKENS, D), jnp.float32)
    return jnp.clip(base * rows * cols * 0.4, -40.0, 40.0).astype(jnp.bfloat16)


def steps_of(own_key, dims, pieces, low, top_value):
    def one(position, blocks):
        steps = jax.random.uniform(jax.random.fold_in(jax.random.fold_in(own_key, 6), position), (blocks,), jnp.float32, low / len(pieces), top_value / len(pieces))
        return jnp.repeat(jnp.exp(steps), dims[position] // blocks).reshape((-1,) + (1,) * (len(dims) - position - 1))

    level = one(*pieces[0])
    for cut in pieces[1:]:
        level = level * one(*cut)
    return level


def scatter_about(rng, shape, scale, limit, pieces=(), kind=jnp.bfloat16):
    array = scale * jax.random.normal(rng, shape, jnp.float32)
    if pieces:
        array = array * steps_of(rng, shape, pieces, -0.22, 0.18)
    return jnp.clip(array, -limit, limit).astype(kind)


def setup_inputs(seed: int = 0) -> dict:
    splits = jax.random.split(jax.random.key(seed), 5)
    return {
        "tokens": draw_tokens(jax.random.fold_in(splits[4], 71), 0),
        "gain": jnp.clip(1.0 + 0.18 * jax.random.normal(splits[1], (D,), jnp.float32), 0.1, 1.9),
        "w_value": scatter_about(splits[2], (D, KV), D ** -0.5, 0.0625, ((0, 512),)),
        "cotangent": scatter_about(splits[3], (TOKENS, KV), 1.0, 6.0, ((0, 64),)),
    }


EPS = 1e-05

def reference(tokens, gain, w_value, cotangent):
    xf = tokens.astype(jnp.float32)
    squares = lax.optimization_barrier(jnp.sum(xf * xf, axis=1))
    scale = lax.rsqrt(squares / D + EPS)
    gains = gain.astype(jnp.float32)
    normed = (xf * scale[:, None] * gains[None, :]).astype(jnp.bfloat16)
    values = jnp.dot(normed, w_value, preferred_element_type=jnp.float32).astype(jnp.bfloat16)
    grad_weight = lax.dot_general(normed, cotangent, (((0,), (0,)), ((), ())), preferred_element_type=jnp.float32)
    grad_normed = lax.dot_general(cotangent, w_value, (((1,), (1,)), ((), ())), preferred_element_type=jnp.float32)
    inner = lax.optimization_barrier(jnp.sum(gains[None, :] * grad_normed * xf, axis=1))
    grad_tokens = scale[:, None] * gains[None, :] * grad_normed - xf * (scale ** 3 * inner / D)[:, None]
    return (values, grad_weight, grad_tokens.astype(jnp.bfloat16))
```

```python
import functools

import jax
import jax.numpy as jnp
from jax import lax
from jax.experimental import pallas as pl
from jax.experimental.pallas import tpu as pltpu
from jax.sharding import PartitionSpec as P

D = 8192
EPS = 1e-05
MESH = pl.DeviceIdType.MESH
F32 = jnp.float32
BF16 = jnp.bfloat16

NZ = 16
NT = 8
ROWS = 512
FEAT = 1024
KV = 1024
OWN = ROWS // NT
NJ = 4
CW = KV // NJ


def kernel(
    x_ref, gain_ref, w_ref, cot_ref,
    val_ref, gw_ref, gt_ref,
    w_all, normed, scale_b, sq_mine, sq_all,
    pv, rv, own_val, gs, s_acc,
    tf, tb, tr, t2, xs, xr, gsend, leaf, chain,
    wz_s, wz_r, wd_s, wd_r, wx_s, wx_r, wf_s, wf_r, sib_s, sib_r,
    sq_s, sq_r, rs_s, rs_r, ag_s, ag_r,
    core_s, core_r, xs_s, xs_r, leaf_s, leaf_r, chain_s, chain_r,
):
    blk = lax.axis_index("blk")
    tp = lax.axis_index("tp")
    xlo = blk // (2 * NZ)
    z = (blk // 2) % NZ
    core = blk % 2
    sign = (1 - 2 * core, 2 * core - 1)

    def at_z(step, other_x=False):
        x = 1 - xlo if other_x else xlo
        return (x * (2 * NZ) + ((z + step + 2 * NZ) % NZ) * 2 + core, tp)

    sibling = (xlo * (2 * NZ) + z * 2 + 1 - core, tp)
    partner = (blk, tp)

    def tp_peer(k):
        return (blk, (tp + k) % NT)

    def copy(src, dst, s, r, dev):
        return pltpu.make_async_remote_copy(
            src_ref=src, dst_ref=dst, send_sem=s, recv_sem=r, device_id=dev, device_id_type=MESH
        )

    barrier = pltpu.get_barrier_semaphore()
    peers = [at_z(0, True), sibling]
    for step in (1, 2, -1, -2):
        peers += [at_z(step), at_z(step, True)]
    peers += [tp_peer(k) for k in range(1, NT)]
    for dev in peers:
        pl.semaphore_signal(barrier, inc=1, device_id=dev, device_id_type=MESH)

    for q in range(ROWS // 128):
        rows = pl.ds(q * 128, 128)
        acc = jnp.zeros((128, 128), F32)
        for n in range(FEAT // 128):
            xf = x_ref[rows, n * 128 : (n + 1) * 128].astype(F32)
            acc += xf * xf
        sq_mine[:, rows] = jnp.sum(acc.T, axis=0, keepdims=True)
    w_all[xlo, z, core] = w_ref[...]
    pl.semaphore_wait(barrier, len(peers))

    def w_origin(i, k):
        return (z - sign[i] * k + 2 * NZ) % NZ

    mine = w_all.at[xlo, z, core]
    first = []
    for k in (2, 1):
        for i in range(2):
            first.append(copy(mine, mine, wz_s.at[i, k], wz_r.at[i, k], at_z(sign[i] * k)))
            first.append(copy(mine, mine, wd_s.at[i, k], wd_r.at[i, k], at_z(sign[i] * k, True)))
    first.append(copy(mine, mine, wx_s, wx_r, at_z(0, True)))
    for c in first:
        c.start()

    def sq_copy(k):
        return copy(sq_mine, sq_all.at[tp], sq_s.at[k], sq_r.at[NT - k], tp_peer(k))

    def sq_recv(k):
        src = (tp + k) % NT
        return copy(sq_mine, sq_all.at[src], sq_s.at[k], sq_r.at[k], tp_peer(k))

    for k in range(1, NT):
        sq_copy(k).start()
    sq_all[tp] = sq_mine[...]

    def w_forward(i, m, far):
        pair = w_all.at[:, w_origin(i, 2 * m), core]
        k = 2 * m + 1 + far
        return copy(pair, pair, wf_s.at[i, k], wz_r.at[i, k], at_z(sign[i] * (1 + far)))

    def w_wait(i, k):
        if k <= 2:
            one = w_all.at[xlo, w_origin(i, k), core]
            two = w_all.at[1 - xlo, w_origin(i, k), core]
            copy(one, one, wz_s.at[i, k], wz_r.at[i, k], partner).wait_recv()
            copy(two, two, wd_s.at[i, k], wd_r.at[i, k], partner).wait_recv()
        else:
            pair = w_all.at[:, w_origin(i, k), core]
            copy(pair, pair, wf_s.at[i, k], wz_r.at[i, k], partner).wait_recv()

    def sib_copy(origin, slot):
        pair = w_all.at[:, origin, core]
        return copy(pair, pair, sib_s.at[slot], sib_r.at[slot], sibling)

    def sib_slot(i, k):
        return w_origin(i, k)

    def to_sibling(i, k):
        o = w_origin(i, k)
        sib_copy(o, o).start()

    forwards = []

    def w_step(m):
        for i in range(2):
            w_wait(i, 2 * m)
            if not (i == 1 and 2 * m + 2 > 6):
                c = w_forward(i, m, 1)
                c.start()
                forwards.append(c)
            c = w_forward(i, m, 0)
            c.start()
            forwards.append(c)
        for i in range(2):
            to_sibling(i, 2 * m)

    def w_leaf(k):
        for i in range(2):
            w_wait(i, k)
            to_sibling(i, k)

    w_step(1)
    other = w_all.at[1 - xlo, z, core]
    copy(other, other, wx_s, wx_r, partner).wait_recv()
    sib_copy(z, z).start()
    w_leaf(1)

    for k in range(1, NT):
        sq_recv(k).wait_recv()
    total = sq_all[0]
    for k in range(1, NT):
        total = total + sq_all[k]
    scale_row = lax.rsqrt(total / D + EPS)
    for q in range(ROWS // 128):
        rows = pl.ds(q * 128, 128)
        sb = jnp.broadcast_to(scale_row[:, q * 128 : (q + 1) * 128], (128, 128)).T
        scale_b[rows, :] = sb

    @pl.loop(0, ROWS // 128)
    def _(q):
        rows = pl.ds(pl.multiple_of(q * 128, 128), 128)
        sb = scale_b[rows, :][:, :1]
        normed[rows, :] = (x_ref[rows, :].astype(F32) * sb * gain_ref[...]).astype(BF16)

    w_step(2)

    for q in range(4):
        part = lax.dot_general(
            normed[:, q * 256 : (q + 1) * 256], cot_ref[...], (((0,), (0,)), ((), ())),
            preferred_element_type=F32,
        )
        tf[q // 2, (q % 2) * 8 : (q % 2) * 8 + 8] = part.reshape(8, 2, 16, KV)

    def core_copy():
        return copy(tb, tr, core_s, core_r, sibling)

    @pl.loop(0, NZ)
    def _(n):
        for h in range(2):
            tb[h, n] = tf[h, n, 1 - core].astype(BF16)

    core_copy().start()
    w_leaf(3)
    w_step(3)

    core_copy().wait_recv()

    def z_at(i, k):
        return (z - sign[i] * k + 2 * NZ) % NZ

    def x_copy(n):
        return copy(xs.at[n], xr.at[n], xs_s.at[n], xs_r.at[n], at_z(0, True))

    order = [(0, 8)] + [(i, k) for k in (7, 6, 5, 4, 3, 2, 1) for i in range(2)] + [(0, 0)]
    for i, k in order:
        n = z_at(i, k)
        xs[n] = (tf[1 - xlo, n, core] + tr[1 - xlo, n].astype(F32)).astype(BF16)
        x_copy(n).start()
    w_leaf(5)

    @pl.loop(0, NZ)
    def _(n):
        t2[n] = tf[xlo, n, core] + tr[xlo, n].astype(F32)

    w_leaf(7)
    w_wait(0, 8)
    to_sibling(0, 8)
    for o in range(NZ):
        pair = w_all.at[:, o, 1 - core]
        copy(pair, pair, sib_s.at[o], sib_r.at[o], sibling).wait_recv()

    def rs_copy(j, k):
        dst = (tp + k) % NT
        src = pv.at[pl.ds(pl.multiple_of(dst * OWN, OWN), OWN), pl.ds(j * CW, CW)]
        return copy(src, rv.at[j, tp], rs_s.at[j, k], rs_r.at[j, NT - k], tp_peer(k))

    def ag_copy(j, k):
        rows = pl.ds(pl.multiple_of(tp * OWN, OWN), OWN)
        dst = val_ref.at[rows, pl.ds(j * CW, CW)]
        return copy(own_val.at[j], dst, ag_s.at[j, k], ag_r.at[j, NT - k], tp_peer(k))

    def partial(j):
        cols = slice(j * CW, (j + 1) * CW)
        wc = w_all[:, :, :, :, cols].reshape(FEAT, CW)

        @pl.loop(0, 2)
        def _(h):
            rows = pl.ds(pl.multiple_of(h * 256, 256), 256)
            pv[rows, cols] = jnp.dot(
                normed[rows, :], wc, preferred_element_type=F32
            ).astype(BF16)

        for k in (1, 2, 3, 5, 6, 7, 4):
            rs_copy(j, k).start()
        rv[j, tp] = pv[pl.ds(pl.multiple_of(tp * OWN, OWN), OWN), cols]

    def reduce(j):
        for k in range(1, NT):
            src = (tp + k) % NT
            copy(rv.at[j, src], rv.at[j, src], rs_s.at[j, k], rs_r.at[j, k], partner).wait_recv()
        v = rv[j, 0].astype(F32)
        for k in range(1, NT):
            v += rv[j, k].astype(F32)
        own_val[j] = v.astype(BF16)
        for k in (1, 2, 3, 5, 6, 7, 4):
            ag_copy(j, k).start()
        val_ref[pl.ds(pl.multiple_of(tp * OWN, OWN), OWN), j * CW : (j + 1) * CW] = own_val[j]

    def gather(j):
        for k in range(1, NT):
            src = (tp + k) % NT
            rows = pl.ds(pl.multiple_of(src * OWN, OWN), OWN)
            dst = val_ref.at[rows, pl.ds(j * CW, CW)]
            copy(dst, dst, ag_s.at[j, k], ag_r.at[j, k], partner).wait_recv()
        cols = slice(j * CW, (j + 1) * CW)
        prod = val_ref[:, cols].astype(F32) * cot_ref[:, cols].astype(F32)
        s = prod[:, :128] + prod[:, 128:]
        if j == 0:
            s_acc[...] = s
        else:
            s_acc[...] += s

    def x_sum(i, k):
        n = z_at(i, k)
        copy(xs.at[n], xr.at[n], xs_s.at[n], xs_r.at[n], partner).wait_recv()
        return t2[n] + xr[n].astype(F32)

    def leaf_copy(i, m):
        return copy(gsend.at[i, 2 * m + 1], leaf.at[i, m], leaf_s.at[i, m], leaf_r.at[i, m], at_z(-sign[i]))

    def chain_copy(i, m):
        return copy(
            gsend.at[i, 2 * m + 2], chain.at[i, m], chain_s.at[i, m], chain_r.at[i, m], at_z(-2 * sign[i])
        )

    def g_leaf(k):
        for i in range(2):
            gsend[i, k] = x_sum(i, k).astype(BF16)
            leaf_copy(i, (k - 1) // 2).start()

    def g_chain(k):
        for i in range(2):
            if k == 8 and i == 1:
                continue
            acc = x_sum(i, k)
            if k < 8:
                m = k // 2
                leaf_copy(i, m).wait_recv()
                acc += leaf[i, m].astype(F32)
                if not (i == 1 and m == 3):
                    chain_copy(i, m).wait_recv()
                    acc += chain[i, m].astype(F32)
            gsend[i, k] = acc.astype(BF16)
            chain_copy(i, k // 2 - 1).start()

    def g_last():
        acc = x_sum(0, 0)
        for i in range(2):
            leaf_copy(i, 0).wait_recv()
            chain_copy(i, 0).wait_recv()
            acc += leaf[i, 0].astype(F32) + chain[i, 0].astype(F32)
        gw_ref[...] = acc

    def grad(q):
        cols = slice(q * 256, (q + 1) * 256)
        wq = w_all[q // 2, (q % 2) * 8 : (q % 2) * 8 + 8].reshape(256, KV)

        @pl.loop(0, 2)
        def _(h):
            rows = pl.ds(pl.multiple_of(h * 256, 256), 256)
            gn = lax.dot_general(
                cot_ref[rows, :], wq, (((1,), (1,)), ((), ())), preferred_element_type=F32
            )
            gs[rows, cols] = scale_b[rows, :][:, :1] * gain_ref[:, cols] * gn

    partial(0)
    partial(1)
    g_chain(8)
    g_leaf(7)
    partial(2)
    partial(3)
    g_leaf(5)
    grad(0)
    g_chain(6)
    reduce(0)
    g_leaf(3)
    g_leaf(1)
    grad(1)
    reduce(1)
    g_chain(4)
    grad(2)
    reduce(2)
    g_chain(2)
    grad(3)
    reduce(3)
    gather(0)
    gather(1)
    g_last()
    gather(2)
    gather(3)

    @pl.loop(0, ROWS // 128)
    def _(q):
        rows = pl.ds(pl.multiple_of(q * 128, 128), 128)
        sb = scale_b[rows, :][:, :1]
        inner = jnp.sum(s_acc[rows, :], axis=1, keepdims=True)
        coef = sb * sb * inner / D
        gt_ref[rows, :] = (gs[rows, :] - x_ref[rows, :].astype(F32) * coef).astype(BF16)

    for c in first + forwards:
        c.wait_send()
    for o in range(NZ):
        sib_copy(o, o).wait_send()
    for k in range(1, NT):
        sq_copy(k).wait_send()
    core_copy().wait_send()
    for n in range(NZ):
        x_copy(n).wait_send()
    for j in range(NJ):
        for k in range(1, NT):
            rs_copy(j, k).wait_send()
            ag_copy(j, k).wait_send()
    for i in range(2):
        for m in range(4):
            leaf_copy(i, m).wait_send()
            if not (i == 1 and m == 3):
                chain_copy(i, m).wait_send()


def on_device(tokens, gain, w_value, cotangent):
    vmem = pl.BlockSpec(memory_space=pltpu.VMEM)
    dma = pltpu.SemaphoreType.DMA
    scratch = [
        pltpu.VMEM((2, NZ, 2, 16, KV), BF16),
        pltpu.VMEM((ROWS, FEAT), BF16),
        pltpu.VMEM((ROWS, 128), F32),
        pltpu.VMEM((1, ROWS), F32),
        pltpu.VMEM((NT, 1, ROWS), F32),
        pltpu.VMEM((ROWS, KV), BF16),
        pltpu.VMEM((NJ, NT, OWN, CW), BF16),
        pltpu.VMEM((NJ, OWN, CW), BF16),
        pltpu.VMEM((ROWS, FEAT), F32),
        pltpu.VMEM((ROWS, 128), F32),
        pltpu.VMEM((2, NZ, 2, 16, KV), F32),
        pltpu.VMEM((2, NZ, 16, KV), BF16),
        pltpu.VMEM((2, NZ, 16, KV), BF16),
        pltpu.VMEM((NZ, 16, KV), F32),
        pltpu.VMEM((NZ, 16, KV), BF16),
        pltpu.VMEM((NZ, 16, KV), BF16),
        pltpu.VMEM((2, 9, 16, KV), BF16),
        pltpu.VMEM((2, 4, 16, KV), BF16),
        pltpu.VMEM((2, 4, 16, KV), BF16),
        dma((2, 9)), dma((2, 9)),
        dma((2, 3)), dma((2, 3)),
        dma, dma,
        dma((2, 9)), dma((2, 9)),
        dma((NZ,)), dma((NZ,)),
        dma((NT,)), dma((NT,)),
        dma((NJ, NT)), dma((NJ, NT)),
        dma((NJ, NT)), dma((NJ, NT)),
        dma, dma,
        dma((NZ,)), dma((NZ,)),
        dma((2, 4)), dma((2, 4)),
        dma((2, 4)), dma((2, 4)),
    ]
    return pl.pallas_call(
        kernel,
        name="value_projection",
        out_shape=(
            jax.ShapeDtypeStruct((ROWS, KV), BF16),
            jax.ShapeDtypeStruct((16, KV), F32),
            jax.ShapeDtypeStruct((ROWS, FEAT), BF16),
        ),
        in_specs=[vmem] * 4,
        out_specs=(vmem,) * 3,
        scratch_shapes=scratch,
        cost_estimate=pl.CostEstimate(
            flops=6 * ROWS * FEAT * KV, bytes_accessed=8 * 2**20, transcendentals=ROWS
        ),
        compiler_params=pltpu.CompilerParams(
            collective_id=0, has_side_effects=True, vmem_limit_bytes=56 * 2**20
        ),
    )(tokens, gain.reshape(1, FEAT), w_value, cotangent)


def solution(mesh):
    return jax.shard_map(
        on_device,
        mesh=mesh,
        in_specs=(P("blk", "tp"), P("tp"), P(("tp", "blk"), None), P("blk", None)),
        out_specs=(P("blk", None), P(("tp", "blk"), None), P("blk", "tp")),
        check_vma=False,
    )
```

```python
import functools

import jax
import jax.numpy as jnp
from jax import lax
from jax.experimental import pallas as pl
from jax.experimental.pallas import tpu as pltpu
from jax.sharding import PartitionSpec as P

D = 8192
EPS = 1e-05
MESH = pl.DeviceIdType.MESH
F32 = jnp.float32
BF16 = jnp.bfloat16

NZ = 16
NT = 8
ROWS = 512
FEAT = 1024
KV = 1024
OWN = ROWS // NT
NY = 4
NJ = 4
CW = KV // NJ
NH = 1
HW = KV // NH
MODE = ("y", "y", "y", "y")


def kernel(
    x_hbm, gain_ref, w_hbm, cot_hbm,
    val_ref, gw_ref, gt_ref,
    x_ref, cot_ref,
    w_all, normed, scale_b, sq_mine, sq_all,
    pv, r1, q2, r2, gs, s_mine, s_all,
    tf, tb, tr, t2, xs, xr, gsend, leaf, chain,
    wz_s, wz_r, wx_s, wx_r, sib_s, sib_r, sq_s, sq_r, st_s, st_r,
    r1_s, r1_r, r2_s, r2_r, a1_s, a1_r, a2_s, a2_r,
    core_s, core_r, xs_s, xs_r, leaf_s, leaf_r, chain_s, chain_r,
    in_sem,
):
    blk = lax.axis_index("blk")
    tp = lax.axis_index("tp")
    xlo = blk // (2 * NZ)
    z = (blk // 2) % NZ
    core = blk % 2
    xhi = tp // NY
    y = tp % NY
    sign = (1 - 2 * core, 2 * core - 1)

    def at_z(step, other_x=False):
        x = 1 - xlo if other_x else xlo
        return (x * (2 * NZ) + ((z + step + 2 * NZ) % NZ) * 2 + core, tp)

    sibling = (xlo * (2 * NZ) + z * 2 + 1 - core, tp)
    partner = at_z(0, True)

    def tp_peer(k):
        return (blk, (tp + k) % NT)

    def y_peer(k):
        return (blk, xhi * NY + (y + k) % NY)

    x_peer = (blk, (1 - xhi) * NY + y)

    def copy(src, dst, s, r, dev):
        return pltpu.make_async_remote_copy(
            src_ref=src, dst_ref=dst, send_sem=s, recv_sem=r, device_id=dev, device_id_type=MESH
        )

    sent = []

    def start(c):
        c.start()
        sent.append(c)

    def arrived(dst, r):
        copy(dst, dst, r, r, partner).wait_recv()

    def quarter(ref, q):
        return ref.at[pl.ds(q * 128, 128)]

    x_in = [
        pltpu.make_async_copy(quarter(x_hbm, q), quarter(x_ref, q), in_sem.at[q]) for q in range(4)
    ]
    w_in = pltpu.make_async_copy(w_hbm, w_all.at[xlo, z, core], in_sem.at[8])
    cot_in = [
        pltpu.make_async_copy(quarter(cot_hbm, q), quarter(cot_ref, q), in_sem.at[4 + q])
        for q in range(4)
    ]
    w_in.start()
    for c in x_in:
        c.start()

    barrier = pltpu.get_barrier_semaphore()
    peers = [partner, sibling]
    for step in (1, 2, -1, -2):
        peers += [at_z(step), at_z(step, True)]
    peers += [tp_peer(k) for k in range(1, NT)]
    for dev in peers:
        pl.semaphore_signal(barrier, inc=1, device_id=dev, device_id_type=MESH)

    for c in cot_in:
        c.start()
    for q in range(ROWS // 128):
        x_in[q].wait()
        rows = pl.ds(q * 128, 128)
        acc = jnp.zeros((128, 128), F32)
        for n in range(FEAT // 128):
            xf = x_ref[rows, n * 128 : (n + 1) * 128].astype(F32)
            acc += xf * xf
        sq_mine[:, rows] = jnp.sum(acc.T, axis=0, keepdims=True)
    w_in.wait()
    pl.semaphore_wait(barrier, len(peers))

    def origin(i, k):
        return (z - sign[i] * k + 2 * NZ) % NZ

    def w_block(h, i, k, other_x=False):
        x = 1 - xlo if other_x else xlo
        return w_all.at[x, origin(i, k), core, :, pl.ds(h * HW, HW)]

    def w_send(h, i, k, step, diag=False):
        b = w_block(h, i, k)
        r = wx_r if diag else wz_r
        s = wx_s if diag else wz_s
        start(copy(b, b, s.at[h, i, k + step], r.at[h, i, k + step], at_z(sign[i] * step, diag)))

    def w_cross(h, i, k):
        b = w_block(h, i, k)
        start(copy(b, b, wx_s.at[h, i, k], wx_r.at[h, i, k], partner))

    def w_wait(h, i, k):
        arrived(w_block(h, i, k), wz_r.at[h, i, k])

    def w_pair(h, i, k):
        arrived(w_block(h, i, k, True), wx_r.at[h, i, k])
        o = origin(i, k)
        b = w_all.at[:, o, core, :, pl.ds(h * HW, HW)]
        start(copy(b, b, sib_s.at[h, o], sib_r.at[h, o], sibling))

    def w_step(m):
        k = 2 * m
        for h in range(NH):
            for i in range(2):
                w_wait(h, i, k)
                if not (i == 1 and m == 3):
                    w_send(h, i, k, 2)
                    if m == 3:
                        w_send(h, i, k, 2, True)
                w_send(h, i, k, 1)
                if m == 3:
                    w_send(h, i, k, 1, True)
            for i in range(2):
                w_cross(h, i, k)
        for h in range(NH):
            for i in range(2):
                w_wait(h, i, k - 1)
                w_cross(h, i, k - 1)

    for h in range(NH):
        for step in (2, 1):
            for i in range(2):
                w_send(h, i, 0, step)
        w_cross(h, 0, 0)

    for k in range(1, NT):
        start(copy(sq_mine, sq_all.at[tp], sq_s.at[k], sq_r.at[NT - k], tp_peer(k)))
    sq_all[tp] = sq_mine[...]

    w_step(1)
    for h in range(NH):
        w_pair(h, 0, 0)

    for k in range(1, NT):
        arrived(sq_all.at[(tp + k) % NT], sq_r.at[k])
    total = sq_all[0]
    for k in range(1, NT):
        total = total + sq_all[k]
    scale_row = lax.rsqrt(total / D + EPS)
    for q in range(ROWS // 128):
        rows = pl.ds(q * 128, 128)
        sb = jnp.broadcast_to(scale_row[:, q * 128 : (q + 1) * 128], (128, 128)).T
        scale_b[rows, :] = sb

    @pl.loop(0, ROWS // 128)
    def _(q):
        rows = pl.ds(pl.multiple_of(q * 128, 128), 128)
        sb = scale_b[rows, :][:, :1]
        normed[rows, :] = (x_ref[rows, :].astype(F32) * sb * gain_ref[...]).astype(BF16)

    w_step(2)
    for h in range(NH):
        for k in (2, 1):
            for i in range(2):
                w_pair(h, i, k)

    for c in cot_in:
        c.wait()

    for q in range(4):
        part = lax.dot_general(
            normed[:, q * 256 : (q + 1) * 256], cot_ref[...], (((0,), (0,)), ((), ())),
            preferred_element_type=F32,
        )
        tf[q // 2, (q % 2) * 8 : (q % 2) * 8 + 8] = part.reshape(8, 2, 16, KV)

    @pl.loop(0, NZ)
    def _(n):
        for h in range(2):
            tb[h, n] = tf[h, n, 1 - core].astype(BF16)

    start(copy(tb, tr, core_s, core_r, sibling))

    w_step(3)
    for h in range(NH):
        for k in (4, 3):
            for i in range(2):
                w_pair(h, i, k)

    arrived(tr, core_r)

    order = [(0, 8)] + [(i, k) for k in (7, 6, 5, 4, 3, 2, 1) for i in range(2)] + [(0, 0)]
    for i, k in order:
        n = origin(i, k)
        xs[n] = (tf[1 - xlo, n, core] + tr[1 - xlo, n].astype(F32)).astype(BF16)
        start(copy(xs.at[n], xr.at[n], xs_s.at[n], xs_r.at[n], partner))

    @pl.loop(0, NZ)
    def _(n):
        t2[n] = tf[xlo, n, core] + tr[xlo, n].astype(F32)

    def w_finish(h):
        for k in (6, 5):
            for i in range(2):
                w_pair(h, i, k)
        for i, k in ((0, 7), (1, 7), (0, 8)):
            w_wait(h, i, k)
            w_pair(h, i, k)
        for o in range(NZ):
            arrived(w_all.at[:, o, 1 - core, :, pl.ds(h * HW, HW)], sib_r.at[h, o])

    def cols_of(j):
        return pl.ds(j * CW, CW)

    def partial(j):
        wc = w_all[:, :, :, :, j * CW : (j + 1) * CW].reshape(FEAT, CW)

        for h in range(2):
            p = jnp.dot(normed[h * 256 : (h + 1) * 256, :], wc, preferred_element_type=F32)
            pv[h, :, :, j * CW : (j + 1) * CW] = p.astype(BF16).reshape(NY, OWN, CW)

        if MODE[j] == "y":
            for k in (1, 3, 2):
                peer = (y + k) % NY
                start(copy(
                    pv.at[:, peer, :, cols_of(j)], r1.at[j, pl.ds(2 * (NY - k), 2)],
                    r1_s.at[j, k], r1_r.at[j, NY - k], y_peer(k),
                ))
        else:
            start(copy(
                pv.at[1 - xhi, :, :, cols_of(j)], r1.at[j, pl.ds(0, NY)],
                r1_s.at[j, 0], r1_r.at[j, 0], x_peer,
            ))

    def step_a(j):
        cols = slice(j * CW, (j + 1) * CW)
        if MODE[j] == "y":
            for k in range(1, NY):
                arrived(r1.at[j, pl.ds(2 * k, 2)], r1_r.at[j, k])
            for g in range(2):
                x = 1 - xhi if g == 0 else xhi
                acc = pv[x, y, :, cols].astype(F32)
                for k in range(1, NY):
                    acc += r1[j, 2 * k + x].astype(F32)
                if g == 0:
                    q2[j, 0] = acc.astype(BF16)
                    start(copy(q2.at[j, 0], r2.at[j, 0], r2_s.at[j, 0], r2_r.at[j, 0], x_peer))
                else:
                    s_part[j] = acc
        else:
            arrived(r1.at[j, pl.ds(0, NY)], r1_r.at[j, 0])
            for k in (1, 3, 2, 0):
                peer = (y + k) % NY
                acc = pv[xhi, peer, :, cols].astype(F32) + r1[j, peer].astype(F32)
                if k:
                    q2[j, k] = acc.astype(BF16)
                    start(copy(
                        q2.at[j, k], r2.at[j, NY - k], r2_s.at[j, k], r2_r.at[j, NY - k], y_peer(k)
                    ))
                else:
                    s_part[j] = acc

    s_part = {}
    s_sum = []

    def step_b(j):
        cols = slice(j * CW, (j + 1) * CW)
        v = s_part[j]
        for k in range(1, NY) if MODE[j] == "x" else (0,):
            arrived(r2.at[j, k], r2_r.at[j, k])
            v = v + r2[j, k].astype(F32)
        val_ref[xhi, y, :, cols] = v.astype(BF16)
        mine = val_ref.at[xhi, y, :, cols_of(j)]
        if MODE[j] == "y":
            start(copy(mine, mine, a1_s.at[j, 0], a1_r.at[j, 0], x_peer))
        else:
            for k in (1, 3, 2):
                start(copy(mine, mine, a1_s.at[j, k], a1_r.at[j, NY - k], y_peer(k)))
        prod = v * cot_ref[pl.ds(pl.multiple_of(tp * OWN, OWN), OWN), cols].astype(F32)
        for n in range(CW // 128):
            part = prod[:, n * 128 : (n + 1) * 128]
            s_sum.append(part)
        if len(s_sum) == NJ * CW // 128:
            acc = functools.reduce(lambda a, b: a + b, s_sum)
            wide = jnp.concatenate([acc, jnp.zeros((128 - OWN, 128), F32)], axis=0)
            s_mine[...] = jnp.sum(wide.T, axis=0, keepdims=True)
            for k in (1, 2, 3, 5, 6, 7, 4):
                start(copy(s_mine, s_all.at[tp], st_s.at[k], st_r.at[NT - k], tp_peer(k)))
            s_all[tp] = s_mine[...]

    def step_c(j):
        if MODE[j] == "y":
            theirs = val_ref.at[1 - xhi, y, :, cols_of(j)]
            arrived(theirs, a1_r.at[j, 0])
            both = val_ref.at[:, y, :, cols_of(j)]
            for k in (1, 3, 2):
                start(copy(both, both, a2_s.at[j, k], a2_r.at[j, NY - k], y_peer(k)))
        else:
            for k in range(1, NY):
                arrived(val_ref.at[xhi, (y + k) % NY, :, cols_of(j)], a1_r.at[j, k])
            four = val_ref.at[xhi, :, :, cols_of(j)]
            start(copy(four, four, a2_s.at[j, 0], a2_r.at[j, 0], x_peer))

    def step_d(j):
        if MODE[j] == "y":
            for k in range(1, NY):
                arrived(val_ref.at[:, (y + k) % NY, :, cols_of(j)], a2_r.at[j, k])
        else:
            arrived(val_ref.at[1 - xhi, :, :, cols_of(j)], a2_r.at[j, 0])

    def x_sum(i, k):
        n = origin(i, k)
        arrived(xr.at[n], xs_r.at[n])
        return t2[n] + xr[n].astype(F32)

    def g_leaf(k):
        m = (k - 1) // 2
        for i in range(2):
            gsend[i, k] = x_sum(i, k).astype(BF16)
            start(copy(gsend.at[i, k], leaf.at[i, m], leaf_s.at[i, m], leaf_r.at[i, m], at_z(-sign[i])))

    def g_chain(k):
        m = k // 2
        for i in range(2):
            if k == 8 and i == 1:
                continue
            acc = x_sum(i, k)
            if k < 8:
                arrived(leaf.at[i, m], leaf_r.at[i, m])
                acc += leaf[i, m].astype(F32)
                if not (i == 1 and m == 3):
                    arrived(chain.at[i, m], chain_r.at[i, m])
                    acc += chain[i, m].astype(F32)
            gsend[i, k] = acc.astype(BF16)
            start(copy(
                gsend.at[i, k], chain.at[i, m - 1], chain_s.at[i, m - 1], chain_r.at[i, m - 1],
                at_z(-2 * sign[i]),
            ))

    def g_last():
        acc = x_sum(0, 0)
        for i in range(2):
            arrived(leaf.at[i, 0], leaf_r.at[i, 0])
            arrived(chain.at[i, 0], chain_r.at[i, 0])
            acc += leaf[i, 0].astype(F32) + chain[i, 0].astype(F32)
        gw_ref[...] = acc

    def grad(q):
        cols = slice(q * 256, (q + 1) * 256)
        wq = w_all[q // 2, (q % 2) * 8 : (q % 2) * 8 + 8].reshape(256, KV)

        @pl.loop(0, 2)
        def _(h):
            rows = pl.ds(pl.multiple_of(h * 256, 256), 256)
            gn = lax.dot_general(
                cot_ref[rows, :], wq, (((1,), (1,)), ((), ())), preferred_element_type=F32
            )
            gs[rows, cols] = scale_b[rows, :][:, :1] * gain_ref[:, cols] * gn

    w_finish(0)
    partial(0)
    partial(1)
    partial(2)
    partial(3)
    g_chain(8)
    g_leaf(7)
    grad(0)
    step_a(0)
    g_leaf(5)
    step_a(1)
    g_chain(6)
    step_b(0)
    g_leaf(3)
    step_a(2)
    step_b(1)
    step_c(0)
    g_leaf(1)
    g_chain(4)
    step_a(3)
    step_b(2)
    step_c(1)
    grad(1)
    step_b(3)
    g_chain(2)
    step_c(2)
    grad(2)
    step_c(3)
    grad(3)

    for k in range(1, NT):
        arrived(s_all.at[(tp + k) % NT], st_r.at[k])
    for t in range(NT):
        rows = slice(t * OWN, (t + 1) * OWN)
        inner = jnp.broadcast_to(s_all[t], (128, 128)).T[:OWN]
        sb = scale_b[rows, :]
        coef = (sb * sb * inner / D)[:, :1]
        gt_ref[rows, :] = (gs[rows, :] - x_ref[rows, :].astype(F32) * coef).astype(BF16)
    g_last()
    for j in range(NJ):
        step_d(j)

    for c in sent:
        c.wait_send()


def hand_over(val_in, gw_in, gt_in, val_out, gw_out, gt_out, sem):
    copies = [pltpu.make_async_copy(gw_in, gw_out, sem.at[8])]
    for q in range(4):
        rows = pl.ds(q * 128, 128)
        copies.append(pltpu.make_async_copy(val_in.at[rows], val_out.at[rows], sem.at[q]))
        copies.append(pltpu.make_async_copy(gt_in.at[rows], gt_out.at[rows], sem.at[4 + q]))
    for c in copies:
        c.start()
    for c in copies:
        c.wait()


def on_device(tokens, gain, w_value, cotangent):
    vmem = pl.BlockSpec(memory_space=pltpu.VMEM)
    dma = pltpu.SemaphoreType.DMA
    hbm = pl.BlockSpec(memory_space=pl.ANY)
    scratch = [
        pltpu.VMEM((ROWS, FEAT), BF16),
        pltpu.VMEM((ROWS, KV), BF16),
        pltpu.VMEM((2, NZ, 2, 16, KV), BF16),
        pltpu.VMEM((ROWS, FEAT), BF16),
        pltpu.VMEM((ROWS, 128), F32),
        pltpu.VMEM((1, ROWS), F32),
        pltpu.VMEM((NT, 1, ROWS), F32),
        pltpu.VMEM((2, NY, OWN, KV), BF16),
        pltpu.VMEM((NJ, 2 * NY, OWN, CW), BF16),
        pltpu.VMEM((NJ, NY, OWN, CW), BF16),
        pltpu.VMEM((NJ, NY, OWN, CW), BF16),
        pltpu.VMEM((ROWS, FEAT), F32),
        pltpu.VMEM((1, 128), F32),
        pltpu.VMEM((NT, 1, 128), F32),
        pltpu.VMEM((2, NZ, 2, 16, KV), F32),
        pltpu.VMEM((2, NZ, 16, KV), BF16),
        pltpu.VMEM((2, NZ, 16, KV), BF16),
        pltpu.VMEM((NZ, 16, KV), F32),
        pltpu.VMEM((NZ, 16, KV), BF16),
        pltpu.VMEM((NZ, 16, KV), BF16),
        pltpu.VMEM((2, 9, 16, KV), BF16),
        pltpu.VMEM((2, 4, 16, KV), BF16),
        pltpu.VMEM((2, 4, 16, KV), BF16),
        dma((NH, 2, 9)), dma((NH, 2, 9)),
        dma((NH, 2, 9)), dma((NH, 2, 9)),
        dma((NH, NZ)), dma((NH, NZ)),
        dma((NT,)), dma((NT,)),
        dma((NT,)), dma((NT,)),
        dma((NJ, NY)), dma((NJ, NY)),
        dma((NJ, NY)), dma((NJ, NY)),
        dma((NJ, NY)), dma((NJ, NY)),
        dma((NJ, NY)), dma((NJ, NY)),
        dma, dma,
        dma((NZ,)), dma((NZ,)),
        dma((2, 4)), dma((2, 4)),
        dma((2, 4)), dma((2, 4)),
        dma((9,)),
    ]
    values, grad_weight, grad_tokens = pl.pallas_call(
        kernel,
        name="value_projection",
        out_shape=(
            pltpu.VMEM((2, NY, OWN, KV), BF16),
            pltpu.VMEM((16, KV), F32),
            pltpu.VMEM((ROWS, FEAT), BF16),
        ),
        in_specs=[hbm, vmem, hbm, hbm],
        out_specs=(vmem,) * 3,
        scratch_shapes=scratch,
        cost_estimate=pl.CostEstimate(
            flops=6 * ROWS * FEAT * KV, bytes_accessed=8 * 2**20, transcendentals=ROWS
        ),
        compiler_params=pltpu.CompilerParams(
            collective_id=0, has_side_effects=True, vmem_limit_bytes=56 * 2**20
        ),
    )(tokens, gain.reshape(1, FEAT), w_value, cotangent)
    return pl.pallas_call(
        hand_over,
        name="hand_over",
        out_shape=(
            jax.ShapeDtypeStruct((ROWS, KV), BF16),
            jax.ShapeDtypeStruct((16, KV), F32),
            jax.ShapeDtypeStruct((ROWS, FEAT), BF16),
        ),
        in_specs=[vmem] * 3,
        out_specs=(hbm,) * 3,
        scratch_shapes=[dma((9,))],
        compiler_params=pltpu.CompilerParams(vmem_limit_bytes=16 * 2**20),
    )(values.reshape(ROWS, KV), grad_weight, grad_tokens)


def solution(mesh):
    return jax.shard_map(
        on_device,
        mesh=mesh,
        in_specs=(P("blk", "tp"), P("tp"), P(("tp", "blk"), None), P("blk", None)),
        out_specs=(P("blk", None), P(("tp", "blk"), None), P("blk", "tp")),
        check_vma=False,
    )
```

```python
import functools

import jax
import jax.numpy as jnp
from jax import lax
from jax.experimental import pallas as pl
from jax.experimental.pallas import tpu as pltpu
from jax.sharding import PartitionSpec as P

D = 8192
EPS = 1e-05
MESH = pl.DeviceIdType.MESH
F32 = jnp.float32
BF16 = jnp.bfloat16

NZ = 16
NT = 8
ROWS = 512
FEAT = 1024
KV = 1024
OWN = ROWS // NT
NY = 4
NJ = 4
CW = KV // NJ
NH = 1
HW = KV // NH
SUM_FIRST = ("y", "y", "y", "y")
SEND_LAST = ("y", "x", "y", "x")


def kernel(
    x_hbm, gain_hbm, w_hbm, cot_hbm,
    val_ref, gw_ref, gt_ref,
    x_ref, cot_ref, gain_ref,
    w_all, normed, scale_b, sq_mine, sq_all,
    pv, r1, q2, r2, gs, s_mine, s_all,
    tf, tb, tr, t2, xs, xr, gsend, leaf, chain,
    wz_s, wz_r, wx_s, wx_r, sib_s, sib_r, sq_s, sq_r, st_s, st_r,
    r1_s, r1_r, r2_s, r2_r, a1_s, a1_r, a2_s, a2_r,
    core_s, core_r, xs_s, xs_r, leaf_s, leaf_r, chain_s, chain_r,
    in_sem,
):
    blk = lax.axis_index("blk")
    tp = lax.axis_index("tp")
    xlo = blk // (2 * NZ)
    z = (blk // 2) % NZ
    core = blk % 2
    xhi = tp // NY
    y = tp % NY
    sign = (1 - 2 * core, 2 * core - 1)

    def at_z(step, other_x=False):
        x = 1 - xlo if other_x else xlo
        return (x * (2 * NZ) + ((z + step + 2 * NZ) % NZ) * 2 + core, tp)

    sibling = (xlo * (2 * NZ) + z * 2 + 1 - core, tp)
    partner = at_z(0, True)

    def tp_peer(k):
        return (blk, (tp + k) % NT)

    def y_peer(k):
        return (blk, xhi * NY + (y + k) % NY)

    x_peer = (blk, (1 - xhi) * NY + y)

    def copy(src, dst, s, r, dev):
        return pltpu.make_async_remote_copy(
            src_ref=src, dst_ref=dst, send_sem=s, recv_sem=r, device_id=dev, device_id_type=MESH
        )

    def start(c):
        c.start()

    def arrived(dst, r):
        copy(dst, dst, r, r, partner).wait_recv()

    def quarter(ref, q):
        return ref.at[pl.ds(q * 128, 128)]

    x_in = [
        pltpu.make_async_copy(quarter(x_hbm, q), quarter(x_ref, q), in_sem.at[q]) for q in range(4)
    ]
    w_in = pltpu.make_async_copy(w_hbm, w_all.at[xlo, z, core], in_sem.at[8])
    cot_in = [
        pltpu.make_async_copy(quarter(cot_hbm, q), quarter(cot_ref, q), in_sem.at[4 + q])
        for q in range(4)
    ]
    gain_in = pltpu.make_async_copy(gain_hbm, gain_ref, in_sem.at[9])
    w_in.start()

    barrier = pltpu.get_barrier_semaphore()
    peers = [partner, sibling]
    for step in (1, 2, -1, -2):
        peers += [at_z(step), at_z(step, True)]
    peers += [at_z(3), at_z(-3)]
    peers += [tp_peer(k) for k in range(1, NT)]
    for dev in peers:
        pl.semaphore_signal(barrier, inc=1, device_id=dev, device_id_type=MESH)
    for c in x_in + [gain_in]:
        c.start()

    pl.semaphore_wait(barrier, len(peers))
    w_in.wait()

    def origin(i, k):
        return (z - sign[i] * k + 2 * NZ) % NZ

    def w_block(h, i, k, other_x=False):
        x = 1 - xlo if other_x else xlo
        return w_all.at[x, origin(i, k), core, :, pl.ds(h * HW, HW)]

    def w_send(h, i, k, step, diag=False):
        b = w_block(h, i, k)
        r = wx_r if diag else wz_r
        s = wz_s
        start(copy(b, b, s.at[h], r.at[h, i, k + step], at_z(sign[i] * step, diag)))

    def w_cross(h, i, k):
        b = w_block(h, i, k)
        start(copy(b, b, wx_s.at[h], wx_r.at[h, i, k], partner))

    def w_wait(h, i, k):
        arrived(w_block(h, i, k), wz_r.at[h, i, k])

    def w_pair(h, i, k):
        arrived(w_block(h, i, k, True), wx_r.at[h, i, k])
        o = origin(i, k)
        b = w_all.at[:, o, core, :, pl.ds(h * HW, HW)]
        start(copy(b, b, sib_s.at[h], sib_r.at[h], sibling))

    def w_step(k):
        last = k == 6
        for h in range(NH):
            for i in range(2):
                w_wait(h, i, k)
                for step in (2, 1) if last else (3, 1, 2):
                    if k + step == 8 and i == 1:
                        continue
                    w_send(h, i, k, step)
                    if last:
                        w_send(h, i, k, step, True)
            for i in range(2):
                w_cross(h, i, k)
        for h in range(NH):
            for near in (k - 2, k - 1):
                for i in range(2):
                    w_wait(h, i, near)
                    w_cross(h, i, near)

    for h in range(NH):
        for step in (3, 1, 2):
            for i in range(2):
                w_send(h, i, 0, step)
        w_cross(h, 0, 0)

    for c in cot_in:
        c.start()
    for q in range(ROWS // 128):
        x_in[q].wait()
        rows = pl.ds(q * 128, 128)
        acc = jnp.zeros((128, 128), F32)
        for n in range(FEAT // 128):
            xf = x_ref[rows, n * 128 : (n + 1) * 128].astype(F32)
            acc += xf * xf
        sq_mine[:, rows] = jnp.sum(acc.T, axis=0, keepdims=True)

    for k in range(1, NT):
        start(copy(sq_mine, sq_all.at[tp], sq_s, sq_r, tp_peer(k)))
    sq_all[tp] = sq_mine[...]

    w_step(3)
    for h in range(NH):
        w_pair(h, 0, 0)

    gain_in.wait()
    arrived(sq_all.at[pl.ds(0, NT - 1)], sq_r)
    total = sq_all[0]
    for k in range(1, NT):
        total = total + sq_all[k]
    scale_row = lax.rsqrt(total / D + EPS)
    for q in range(ROWS // 128):
        rows = pl.ds(q * 128, 128)
        sb = jnp.broadcast_to(scale_row[:, q * 128 : (q + 1) * 128], (128, 128)).T
        scale_b[rows, :] = sb

    @pl.loop(0, ROWS // 128)
    def _(q):
        rows = pl.ds(pl.multiple_of(q * 128, 128), 128)
        sb = scale_b[rows, :][:, :1]
        normed[rows, :] = (x_ref[rows, :].astype(F32) * sb * gain_ref[...]).astype(BF16)

    w_step(6)
    for h in range(NH):
        for k in (3, 1, 2):
            for i in range(2):
                w_pair(h, i, k)

    for c in cot_in:
        c.wait()

    for q in range(4):
        part = lax.dot_general(
            normed[:, q * 256 : (q + 1) * 256], cot_ref[...], (((0,), (0,)), ((), ())),
            preferred_element_type=F32,
        )
        tf[q // 2, (q % 2) * 8 : (q % 2) * 8 + 8] = part.reshape(8, 2, 16, KV)

    @pl.loop(0, NZ)
    def _(n):
        for h in range(2):
            tb[h, n] = tf[h, n, 1 - core].astype(BF16)

    start(copy(tb, tr, core_s, core_r, sibling))

    arrived(tr, core_r)

    order = [(0, 8)] + [(i, k) for k in (7, 6, 5, 4, 3, 2, 1) for i in range(2)] + [(0, 0)]
    for i, k in order:
        n = origin(i, k)
        xs[n] = (tf[1 - xlo, n, core] + tr[1 - xlo, n].astype(F32)).astype(BF16)
        start(copy(xs.at[n], xr.at[n], xs_s, xs_r.at[n], partner))

    @pl.loop(0, NZ)
    def _(n):
        t2[n] = tf[xlo, n, core] + tr[xlo, n].astype(F32)

    def w_finish(h):
        for k in (6, 4, 5):
            for i in range(2):
                w_pair(h, i, k)
        for i, k in ((0, 7), (1, 7), (0, 8)):
            w_wait(h, i, k)
            w_pair(h, i, k)
        arrived(w_all.at[:, :, 1 - core, :, pl.ds(h * HW, HW)], sib_r.at[h])

    def cols_of(j):
        return pl.ds(j * CW, CW)

    def partial(j):
        wc = w_all[:, :, :, :, j * CW : (j + 1) * CW].reshape(FEAT, CW)

        for h in range(2):
            p = jnp.dot(normed[h * 256 : (h + 1) * 256, :], wc, preferred_element_type=F32)
            pv[h, :, :, j * CW : (j + 1) * CW] = p.astype(BF16).reshape(NY, OWN, CW)

        if SUM_FIRST[j] == "y":
            for k in (1, 3, 2):
                peer = (y + k) % NY
                start(copy(
                    pv.at[:, peer, :, cols_of(j)], r1.at[j, pl.ds(2 * (NY - k), 2)],
                    r1_s, r1_r.at[j], y_peer(k),
                ))
        else:
            start(copy(
                pv.at[1 - xhi, :, :, cols_of(j)], r1.at[j, pl.ds(0, NY)],
                r1_s, r1_r.at[j], x_peer,
            ))

    def step_a(j):
        cols = slice(j * CW, (j + 1) * CW)
        if SUM_FIRST[j] == "y":
            arrived(r1.at[j, pl.ds(2, 2 * NY - 2)], r1_r.at[j])
            for g in range(2):
                x = 1 - xhi if g == 0 else xhi
                acc = pv[x, y, :, cols].astype(F32)
                for k in range(1, NY):
                    acc += r1[j, 2 * k + x].astype(F32)
                if g == 0:
                    q2[j, 0] = acc.astype(BF16)
                    start(copy(q2.at[j, 0], r2.at[j, 0], r2_s, r2_r.at[j], x_peer))
                else:
                    s_part[j] = acc
        else:
            arrived(r1.at[j, pl.ds(0, NY)], r1_r.at[j])
            for k in (1, 3, 2, 0):
                peer = (y + k) % NY
                acc = pv[xhi, peer, :, cols].astype(F32) + r1[j, peer].astype(F32)
                if k:
                    q2[j, k] = acc.astype(BF16)
                    start(copy(
                        q2.at[j, k], r2.at[j, NY - k], r2_s, r2_r.at[j], y_peer(k)
                    ))
                else:
                    s_part[j] = acc

    s_part = {}
    s_sum = []

    def step_b(j):
        cols = slice(j * CW, (j + 1) * CW)
        v = s_part[j]
        slots = (0, 1) if SUM_FIRST[j] == "y" else (1, NY)
        arrived(r2.at[j, pl.ds(slots[0], slots[1] - slots[0])], r2_r.at[j])
        for k in range(*slots):
            v = v + r2[j, k].astype(F32)
        val_ref[xhi, y, :, cols] = v.astype(BF16)
        mine = val_ref.at[xhi, y, :, cols_of(j)]
        if SEND_LAST[j] == "y":
            start(copy(mine, mine, a1_s, a1_r.at[j], x_peer))
        else:
            for k in (1, 3, 2):
                start(copy(mine, mine, a1_s, a1_r.at[j], y_peer(k)))
        prod = v * cot_ref[pl.ds(pl.multiple_of(tp * OWN, OWN), OWN), cols].astype(F32)
        for n in range(CW // 128):
            part = prod[:, n * 128 : (n + 1) * 128]
            s_sum.append(part)
        if len(s_sum) == NJ * CW // 128:
            acc = functools.reduce(lambda a, b: a + b, s_sum)
            wide = jnp.concatenate([acc, jnp.zeros((128 - OWN, 128), F32)], axis=0)
            s_mine[...] = jnp.sum(wide.T, axis=0, keepdims=True)
            for k in (1, 2, 3, 5, 6, 7, 4):
                start(copy(s_mine, s_all.at[tp], st_s, st_r, tp_peer(k)))
            s_all[tp] = s_mine[...]

    def step_c(j):
        if SEND_LAST[j] == "y":
            theirs = val_ref.at[1 - xhi, y, :, cols_of(j)]
            arrived(theirs, a1_r.at[j])
            both = val_ref.at[:, y, :, cols_of(j)]
            for k in (1, 3, 2):
                start(copy(both, both, a2_s, a2_r.at[j], y_peer(k)))
        else:
            arrived(val_ref.at[0, pl.ds(0, NY - 1), :, cols_of(j)], a1_r.at[j])
            four = val_ref.at[xhi, :, :, cols_of(j)]
            start(copy(four, four, a2_s, a2_r.at[j], x_peer))

    def step_d(j):
        if SEND_LAST[j] == "y":
            arrived(val_ref.at[:, pl.ds(0, NY - 1), :, cols_of(j)], a2_r.at[j])
        else:
            arrived(val_ref.at[1 - xhi, :, :, cols_of(j)], a2_r.at[j])

    def x_sum(i, k):
        n = origin(i, k)
        arrived(xr.at[n], xs_r.at[n])
        return t2[n] + xr[n].astype(F32)

    def g_leaf(k):
        m = (k - 1) // 2
        for i in range(2):
            gsend[i, k] = x_sum(i, k).astype(BF16)
            start(copy(gsend.at[i, k], leaf.at[i, m], leaf_s, leaf_r.at[i, m], at_z(-sign[i])))

    def g_chain(k):
        m = k // 2
        for i in range(2):
            if k == 8 and i == 1:
                continue
            acc = x_sum(i, k)
            if k < 8:
                arrived(leaf.at[i, m], leaf_r.at[i, m])
                acc += leaf[i, m].astype(F32)
                if not (i == 1 and m == 3):
                    arrived(chain.at[i, m], chain_r.at[i, m])
                    acc += chain[i, m].astype(F32)
            gsend[i, k] = acc.astype(BF16)
            start(copy(
                gsend.at[i, k], chain.at[i, m - 1], chain_s, chain_r.at[i, m - 1],
                at_z(-2 * sign[i]),
            ))

    def g_last():
        acc = x_sum(0, 0)
        for i in range(2):
            arrived(leaf.at[i, 0], leaf_r.at[i, 0])
            arrived(chain.at[i, 0], chain_r.at[i, 0])
            acc += leaf[i, 0].astype(F32) + chain[i, 0].astype(F32)
        gw_ref[...] = acc

    def grad(q):
        cols = slice(q * 256, (q + 1) * 256)
        wq = w_all[q // 2, (q % 2) * 8 : (q % 2) * 8 + 8].reshape(256, KV)

        @pl.loop(0, 2)
        def _(h):
            rows = pl.ds(pl.multiple_of(h * 256, 256), 256)
            gn = lax.dot_general(
                cot_ref[rows, :], wq, (((1,), (1,)), ((), ())), preferred_element_type=F32
            )
            gs[rows, cols] = scale_b[rows, :][:, :1] * gain_ref[:, cols] * gn

    w_finish(0)
    partial(0)
    partial(1)
    partial(2)
    partial(3)
    g_chain(8)
    g_leaf(7)
    grad(0)
    step_a(0)
    g_leaf(5)
    step_a(1)
    g_chain(6)
    step_b(0)
    g_leaf(3)
    step_a(2)
    step_b(1)
    step_c(0)
    g_leaf(1)
    g_chain(4)
    step_a(3)
    step_b(2)
    step_c(1)
    grad(1)
    step_b(3)
    g_chain(2)
    step_c(2)
    grad(2)
    step_c(3)
    grad(3)

    arrived(s_all.at[pl.ds(0, NT - 1)], st_r)
    for t in range(NT):
        rows = slice(t * OWN, (t + 1) * OWN)
        inner = jnp.broadcast_to(s_all[t], (128, 128)).T[:OWN]
        sb = scale_b[rows, :]
        coef = (sb * sb * inner / D)[:, :1]
        gt_ref[rows, :] = (gs[rows, :] - x_ref[rows, :].astype(F32) * coef).astype(BF16)
    g_last()
    for j in range(NJ):
        step_d(j)

    def left(ref, s):
        copy(ref, ref, s, s, partner).wait_send()

    left(sq_all.at[pl.ds(0, NT - 1)], sq_s)
    left(s_all.at[pl.ds(0, NT - 1)], st_s)
    for h in range(NH):
        part = pl.ds(h * HW, HW)
        left(w_all.at[0, pl.ds(0, 9), :, :, part], wz_s.at[h])
        left(w_all.at[0, pl.ds(0, 13), 0, :, part], wx_s.at[h])
        left(w_all.at[:, :, 0, :, part], sib_s.at[h])
    left(tb, core_s)
    left(xs, xs_s)
    left(leaf, leaf_s)
    left(gsend.at[0, pl.ds(0, 7)], chain_s)
    first = sum(6 if m == "y" else 4 for m in SUM_FIRST)
    left(r1.at[:, pl.ds(0, first // NJ)], r1_s)
    second = sum(1 if m == "y" else 3 for m in SUM_FIRST)
    left(r1.at[:, pl.ds(0, second // NJ)], r2_s)
    third = sum(1 if m == "y" else 3 for m in SEND_LAST)
    left(r1.at[:, pl.ds(0, third // NJ)], a1_s)
    fourth = sum(6 if m == "y" else 4 for m in SEND_LAST)
    left(r1.at[:, pl.ds(0, fourth // NJ)], a2_s)


def hand_over(val_in, gw_in, gt_in, val_out, gw_out, gt_out, sem):
    copies = [pltpu.make_async_copy(gw_in, gw_out, sem.at[8])]
    for q in range(4):
        rows = pl.ds(q * 128, 128)
        copies.append(pltpu.make_async_copy(val_in.at[rows], val_out.at[rows], sem.at[q]))
        copies.append(pltpu.make_async_copy(gt_in.at[rows], gt_out.at[rows], sem.at[4 + q]))
    for c in copies:
        c.start()
    for c in copies:
        c.wait()


def on_device(tokens, gain, w_value, cotangent):
    vmem = pl.BlockSpec(memory_space=pltpu.VMEM)
    dma = pltpu.SemaphoreType.DMA
    hbm = pl.BlockSpec(memory_space=pl.ANY)
    scratch = [
        pltpu.VMEM((ROWS, FEAT), BF16),
        pltpu.VMEM((ROWS, KV), BF16),
        pltpu.VMEM((1, FEAT), F32),
        pltpu.VMEM((2, NZ, 2, 16, KV), BF16),
        pltpu.VMEM((ROWS, FEAT), BF16),
        pltpu.VMEM((ROWS, 128), F32),
        pltpu.VMEM((1, ROWS), F32),
        pltpu.VMEM((NT, 1, ROWS), F32),
        pltpu.VMEM((2, NY, OWN, KV), BF16),
        pltpu.VMEM((NJ, 2 * NY, OWN, CW), BF16),
        pltpu.VMEM((NJ, NY, OWN, CW), BF16),
        pltpu.VMEM((NJ, NY, OWN, CW), BF16),
        pltpu.VMEM((ROWS, FEAT), F32),
        pltpu.VMEM((1, 128), F32),
        pltpu.VMEM((NT, 1, 128), F32),
        pltpu.VMEM((2, NZ, 2, 16, KV), F32),
        pltpu.VMEM((2, NZ, 16, KV), BF16),
        pltpu.VMEM((2, NZ, 16, KV), BF16),
        pltpu.VMEM((NZ, 16, KV), F32),
        pltpu.VMEM((NZ, 16, KV), BF16),
        pltpu.VMEM((NZ, 16, KV), BF16),
        pltpu.VMEM((2, 9, 16, KV), BF16),
        pltpu.VMEM((2, 4, 16, KV), BF16),
        pltpu.VMEM((2, 4, 16, KV), BF16),
        dma((NH,)), dma((NH, 2, 9)),
        dma((NH,)), dma((NH, 2, 9)),
        dma((NH,)), dma((NH,)),
        dma, dma,
        dma, dma,
        dma, dma((NJ,)),
        dma, dma((NJ,)),
        dma, dma((NJ,)),
        dma, dma((NJ,)),
        dma, dma,
        dma, dma((NZ,)),
        dma, dma((2, 4)),
        dma, dma((2, 4)),
        dma((10,)),
    ]
    values, grad_weight, grad_tokens = pl.pallas_call(
        kernel,
        name="value_projection",
        out_shape=(
            pltpu.VMEM((2, NY, OWN, KV), BF16),
            pltpu.VMEM((16, KV), F32),
            pltpu.VMEM((ROWS, FEAT), BF16),
        ),
        in_specs=[hbm] * 4,
        out_specs=(vmem,) * 3,
        scratch_shapes=scratch,
        cost_estimate=pl.CostEstimate(
            flops=6 * ROWS * FEAT * KV, bytes_accessed=8 * 2**20, transcendentals=ROWS
        ),
        compiler_params=pltpu.CompilerParams(
            collective_id=0, has_side_effects=True, vmem_limit_bytes=56 * 2**20
        ),
    )(tokens, gain.reshape(1, FEAT), w_value, cotangent)
    return pl.pallas_call(
        hand_over,
        name="hand_over",
        out_shape=(
            jax.ShapeDtypeStruct((ROWS, KV), BF16),
            jax.ShapeDtypeStruct((16, KV), F32),
            jax.ShapeDtypeStruct((ROWS, FEAT), BF16),
        ),
        in_specs=[vmem] * 3,
        out_specs=(hbm,) * 3,
        scratch_shapes=[dma((9,))],
        compiler_params=pltpu.CompilerParams(vmem_limit_bytes=16 * 2**20),
    )(values.reshape(ROWS, KV), grad_weight, grad_tokens)


def solution(mesh):
    return jax.shard_map(
        on_device,
        mesh=mesh,
        in_specs=(P("blk", "tp"), P("tp"), P(("tp", "blk"), None), P("blk", None)),
        out_specs=(P("blk", None), P(("tp", "blk"), None), P("blk", "tp")),
        check_vma=False,
    )
```

```python
import functools

import jax
import jax.numpy as jnp
from jax import lax
from jax.experimental import pallas as pl
from jax.experimental.pallas import tpu as pltpu
from jax.sharding import PartitionSpec as P

D = 8192
EPS = 1e-05
MESH = pl.DeviceIdType.MESH
F32 = jnp.float32
BF16 = jnp.bfloat16

NZ = 16
NT = 8
ROWS = 512
FEAT = 1024
KV = 1024
OWN = ROWS // NT
NY = 4
NJ = 4
CW = KV // NJ
NH = 1
HW = KV // NH
SUM_FIRST = ("y", "y", "y", "y")
SEND_LAST = ("y", "x", "y", "x")


def kernel(
    x_hbm, gain_hbm, w_hbm, cot_hbm,
    val_ref, gw_ref, gt_ref,
    x_ref, cot_ref, gain_ref,
    w_all, normed, scale_b, sq_mine, sq_all,
    pv, r1, q2, r2, gs, s_mine, s_all,
    tf, tb, tr, t2, xs, xr, gsend, leaf, chain,
    wz_s, wz_r, wx_s, wx_r, sib_s, sib_r, sq_s, sq_r, st_s, st_r,
    r1_s, r1_r, r2_s, r2_r, a1_s, a1_r, a2_s, a2_r,
    core_s, core_r, xs_s, xs_r, leaf_s, leaf_r, chain_s, chain_r,
    in_sem,
):
    blk = lax.axis_index("blk")
    tp = lax.axis_index("tp")
    xlo = blk // (2 * NZ)
    z = (blk // 2) % NZ
    core = blk % 2
    xhi = tp // NY
    y = tp % NY
    sign = (1 - 2 * core, 2 * core - 1)

    def at_z(step, other_x=False):
        x = 1 - xlo if other_x else xlo
        return (x * (2 * NZ) + ((z + step + 2 * NZ) % NZ) * 2 + core, tp)

    sibling = (xlo * (2 * NZ) + z * 2 + 1 - core, tp)
    partner = at_z(0, True)

    def tp_peer(k):
        return (blk, (tp + k) % NT)

    def y_peer(k):
        return (blk, xhi * NY + (y + k) % NY)

    x_peer = (blk, (1 - xhi) * NY + y)

    def copy(src, dst, s, r, dev):
        return pltpu.make_async_remote_copy(
            src_ref=src, dst_ref=dst, send_sem=s, recv_sem=r, device_id=dev, device_id_type=MESH
        )

    def start(c):
        c.start()

    def arrived(dst, r):
        copy(dst, dst, r, r, partner).wait_recv()

    def quarter(ref, q):
        return ref.at[pl.ds(q * 128, 128)]

    x_in = [
        pltpu.make_async_copy(quarter(x_hbm, q), quarter(x_ref, q), in_sem.at[q]) for q in range(4)
    ]
    w_in = pltpu.make_async_copy(w_hbm, w_all.at[xlo, z, core], in_sem.at[8])
    cot_in = [
        pltpu.make_async_copy(quarter(cot_hbm, q), quarter(cot_ref, q), in_sem.at[4 + q])
        for q in range(4)
    ]
    gain_in = pltpu.make_async_copy(gain_hbm, gain_ref, in_sem.at[9])
    w_in.start()

    barrier = pltpu.get_barrier_semaphore()
    peers = [partner, sibling]
    for step in (1, 2, -1, -2):
        peers += [at_z(step), at_z(step, True)]
    peers += [at_z(3), at_z(-3)]
    peers += [tp_peer(k) for k in range(1, NT)]
    for dev in peers:
        pl.semaphore_signal(barrier, inc=1, device_id=dev, device_id_type=MESH)
    for c in x_in + [gain_in]:
        c.start()

    pl.semaphore_wait(barrier, len(peers))
    w_in.wait()

    def origin(i, k):
        return (z - sign[i] * k + 2 * NZ) % NZ

    def w_block(h, i, k, other_x=False):
        x = 1 - xlo if other_x else xlo
        return w_all.at[x, origin(i, k), core, :, pl.ds(h * HW, HW)]

    def w_send(h, i, k, step, diag=False):
        b = w_block(h, i, k)
        r = wx_r if diag else wz_r
        s = wz_s
        start(copy(b, b, s.at[h], r.at[h, i, k + step], at_z(sign[i] * step, diag)))

    def w_cross(h, i, k):
        b = w_block(h, i, k)
        start(copy(b, b, wx_s.at[h], wx_r.at[h, i, k], partner))

    def w_wait(h, i, k):
        arrived(w_block(h, i, k), wz_r.at[h, i, k])

    def w_pair(h, i, k):
        arrived(w_block(h, i, k, True), wx_r.at[h, i, k])
        o = origin(i, k)
        b = w_all.at[:, o, core, :, pl.ds(h * HW, HW)]
        start(copy(b, b, sib_s.at[h], sib_r.at[h], sibling))

    def w_step(k):
        last = k == 6
        for h in range(NH):
            for i in range(2):
                w_wait(h, i, k)
                for step in (2, 1) if last else (3, 1, 2):
                    if k + step == 8 and i == 1:
                        continue
                    w_send(h, i, k, step)
                    if last:
                        w_send(h, i, k, step, True)
            for i in range(2):
                w_cross(h, i, k)
        for h in range(NH):
            for near in (k - 2, k - 1):
                for i in range(2):
                    w_wait(h, i, near)
                    w_cross(h, i, near)

    for h in range(NH):
        for step in (3, 1, 2):
            for i in range(2):
                w_send(h, i, 0, step)
        w_cross(h, 0, 0)

    for c in cot_in:
        c.start()
    for q in range(ROWS // 128):
        x_in[q].wait()
        rows = pl.ds(q * 128, 128)
        acc = jnp.zeros((128, 128), F32)
        for n in range(FEAT // 128):
            xf = x_ref[rows, n * 128 : (n + 1) * 128].astype(F32)
            acc += xf * xf
        sq_mine[:, rows] = jnp.sum(acc.T, axis=0, keepdims=True)

    for k in range(1, NT):
        start(copy(sq_mine, sq_all.at[tp], sq_s, sq_r, tp_peer(k)))
    sq_all[tp] = sq_mine[...]

    w_step(3)
    for h in range(NH):
        w_pair(h, 0, 0)

    gain_in.wait()
    arrived(sq_all.at[pl.ds(0, NT - 1)], sq_r)
    total = sq_all[0]
    for k in range(1, NT):
        total = total + sq_all[k]
    scale_row = lax.rsqrt(total / D + EPS)
    for q in range(ROWS // 128):
        rows = pl.ds(q * 128, 128)
        sb = jnp.broadcast_to(scale_row[:, q * 128 : (q + 1) * 128], (128, 128)).T
        scale_b[rows, :] = sb

    @pl.loop(0, ROWS // 128)
    def _(q):
        rows = pl.ds(pl.multiple_of(q * 128, 128), 128)
        sb = scale_b[rows, :][:, :1]
        normed[rows, :] = (x_ref[rows, :].astype(F32) * sb * gain_ref[...]).astype(BF16)

    w_step(6)

    def term(first):
        x = 1 - xlo if first else xlo
        for q in range(2):
            cols = pl.ds(pl.multiple_of(x * (FEAT // 2) + q * 256, 256), 256)
            part = lax.dot_general(
                normed[:, cols], cot_ref[...], (((0,), (0,)), ((), ())), preferred_element_type=F32
            )
            tf[x, q * 8 : q * 8 + 8] = part.reshape(8, 2, 16, KV)

        @pl.loop(0, NZ)
        def _(n):
            tb[x, n] = tf[x, n, 1 - core].astype(BF16)

        slot = 0 if first else 1
        start(copy(tb.at[x], tr.at[x], core_s.at[slot], core_r.at[slot], sibling))

    for c in cot_in:
        c.wait()
    term(True)
    term(False)

    for h in range(NH):
        for k in (3, 1, 2):
            for i in range(2):
                w_pair(h, i, k)

    arrived(tr.at[1 - xlo], core_r.at[0])

    order = [(0, 8)] + [(i, k) for k in (7, 6, 5, 4, 3, 2, 1) for i in range(2)] + [(0, 0)]
    for i, k in order:
        n = origin(i, k)
        xs[n] = (tf[1 - xlo, n, core] + tr[1 - xlo, n].astype(F32)).astype(BF16)
        start(copy(xs.at[n], xr.at[n], xs_s, xs_r.at[n], partner))

    arrived(tr.at[xlo], core_r.at[1])

    @pl.loop(0, NZ)
    def _(n):
        t2[n] = tf[xlo, n, core] + tr[xlo, n].astype(F32)

    def w_finish(h):
        for k in (6, 4, 5):
            for i in range(2):
                w_pair(h, i, k)
        for i, k in ((0, 7), (1, 7), (0, 8)):
            w_wait(h, i, k)
            w_pair(h, i, k)
        arrived(w_all.at[:, :, 1 - core, :, pl.ds(h * HW, HW)], sib_r.at[h])

    def cols_of(j):
        return pl.ds(j * CW, CW)

    def partial(j):
        wc = w_all[:, :, :, :, j * CW : (j + 1) * CW].reshape(FEAT, CW)

        for h in range(2):
            p = jnp.dot(normed[h * 256 : (h + 1) * 256, :], wc, preferred_element_type=F32)
            pv[h, :, :, j * CW : (j + 1) * CW] = p.astype(BF16).reshape(NY, OWN, CW)

        if SUM_FIRST[j] == "y":
            for k in (1, 3, 2):
                peer = (y + k) % NY
                start(copy(
                    pv.at[:, peer, :, cols_of(j)], r1.at[j, pl.ds(2 * (NY - k), 2)],
                    r1_s, r1_r.at[j], y_peer(k),
                ))
        else:
            start(copy(
                pv.at[1 - xhi, :, :, cols_of(j)], r1.at[j, pl.ds(0, NY)],
                r1_s, r1_r.at[j], x_peer,
            ))

    def step_a(j):
        cols = slice(j * CW, (j + 1) * CW)
        if SUM_FIRST[j] == "y":
            arrived(r1.at[j, pl.ds(2, 2 * NY - 2)], r1_r.at[j])
            for g in range(2):
                x = 1 - xhi if g == 0 else xhi
                acc = pv[x, y, :, cols].astype(F32)
                for k in range(1, NY):
                    acc += r1[j, 2 * k + x].astype(F32)
                if g == 0:
                    q2[j, 0] = acc.astype(BF16)
                    start(copy(q2.at[j, 0], r2.at[j, 0], r2_s, r2_r.at[j], x_peer))
                else:
                    s_part[j] = acc
        else:
            arrived(r1.at[j, pl.ds(0, NY)], r1_r.at[j])
            for k in (1, 3, 2, 0):
                peer = (y + k) % NY
                acc = pv[xhi, peer, :, cols].astype(F32) + r1[j, peer].astype(F32)
                if k:
                    q2[j, k] = acc.astype(BF16)
                    start(copy(
                        q2.at[j, k], r2.at[j, NY - k], r2_s, r2_r.at[j], y_peer(k)
                    ))
                else:
                    s_part[j] = acc

    s_part = {}
    s_sum = []

    def step_b(j):
        cols = slice(j * CW, (j + 1) * CW)
        v = s_part[j]
        slots = (0, 1) if SUM_FIRST[j] == "y" else (1, NY)
        arrived(r2.at[j, pl.ds(slots[0], slots[1] - slots[0])], r2_r.at[j])
        for k in range(*slots):
            v = v + r2[j, k].astype(F32)
        val_ref[xhi, y, :, cols] = v.astype(BF16)
        mine = val_ref.at[xhi, y, :, cols_of(j)]
        if SEND_LAST[j] == "y":
            start(copy(mine, mine, a1_s, a1_r.at[j], x_peer))
        else:
            for k in (1, 3, 2):
                start(copy(mine, mine, a1_s, a1_r.at[j], y_peer(k)))
        prod = v * cot_ref[pl.ds(pl.multiple_of(tp * OWN, OWN), OWN), cols].astype(F32)
        for n in range(CW // 128):
            part = prod[:, n * 128 : (n + 1) * 128]
            s_sum.append(part)
        if len(s_sum) == NJ * CW // 128:
            acc = functools.reduce(lambda a, b: a + b, s_sum)
            wide = jnp.concatenate([acc, jnp.zeros((128 - OWN, 128), F32)], axis=0)
            s_mine[...] = jnp.sum(wide.T, axis=0, keepdims=True)
            for k in (1, 2, 3, 5, 6, 7, 4):
                start(copy(s_mine, s_all.at[tp], st_s, st_r, tp_peer(k)))
            s_all[tp] = s_mine[...]

    def step_c(j):
        if SEND_LAST[j] == "y":
            theirs = val_ref.at[1 - xhi, y, :, cols_of(j)]
            arrived(theirs, a1_r.at[j])
            both = val_ref.at[:, y, :, cols_of(j)]
            for k in (1, 3, 2):
                start(copy(both, both, a2_s, a2_r.at[j], y_peer(k)))
        else:
            arrived(val_ref.at[0, pl.ds(0, NY - 1), :, cols_of(j)], a1_r.at[j])
            four = val_ref.at[xhi, :, :, cols_of(j)]
            start(copy(four, four, a2_s, a2_r.at[j], x_peer))

    def step_d(j):
        if SEND_LAST[j] == "y":
            arrived(val_ref.at[:, pl.ds(0, NY - 1), :, cols_of(j)], a2_r.at[j])
        else:
            arrived(val_ref.at[1 - xhi, :, :, cols_of(j)], a2_r.at[j])

    def x_sum(i, k):
        n = origin(i, k)
        arrived(xr.at[n], xs_r.at[n])
        return t2[n] + xr[n].astype(F32)

    def g_leaf(k):
        m = (k - 1) // 2
        for i in range(2):
            gsend[i, k] = x_sum(i, k).astype(BF16)
            start(copy(gsend.at[i, k], leaf.at[i, m], leaf_s, leaf_r.at[i, m], at_z(-sign[i])))

    def g_chain(k):
        m = k // 2
        for i in range(2):
            if k == 8 and i == 1:
                continue
            acc = x_sum(i, k)
            if k < 8:
                arrived(leaf.at[i, m], leaf_r.at[i, m])
                acc += leaf[i, m].astype(F32)
                if not (i == 1 and m == 3):
                    arrived(chain.at[i, m], chain_r.at[i, m])
                    acc += chain[i, m].astype(F32)
            gsend[i, k] = acc.astype(BF16)
            start(copy(
                gsend.at[i, k], chain.at[i, m - 1], chain_s, chain_r.at[i, m - 1],
                at_z(-2 * sign[i]),
            ))

    def g_last():
        acc = x_sum(0, 0)
        for i in range(2):
            arrived(leaf.at[i, 0], leaf_r.at[i, 0])
            arrived(chain.at[i, 0], chain_r.at[i, 0])
            acc += leaf[i, 0].astype(F32) + chain[i, 0].astype(F32)
        gw_ref[...] = acc

    def grad(q):
        cols = slice(q * 256, (q + 1) * 256)
        wq = w_all[q // 2, (q % 2) * 8 : (q % 2) * 8 + 8].reshape(256, KV)

        @pl.loop(0, 2)
        def _(h):
            rows = pl.ds(pl.multiple_of(h * 256, 256), 256)
            gn = lax.dot_general(
                cot_ref[rows, :], wq, (((1,), (1,)), ((), ())), preferred_element_type=F32
            )
            gs[rows, cols] = scale_b[rows, :][:, :1] * gain_ref[:, cols] * gn

    w_finish(0)
    partial(0)
    partial(1)
    partial(2)
    partial(3)
    g_chain(8)
    g_leaf(7)
    grad(0)
    grad(1)
    step_a(0)
    step_a(1)
    g_chain(6)
    g_leaf(5)
    step_b(0)
    step_a(2)
    step_b(1)
    step_c(0)
    g_leaf(3)
    step_a(3)
    step_b(2)
    step_c(1)
    g_chain(4)
    g_leaf(1)
    step_b(3)
    step_c(2)
    g_chain(2)
    step_c(3)
    grad(2)
    grad(3)

    arrived(s_all.at[pl.ds(0, NT - 1)], st_r)
    for t in range(NT):
        rows = slice(t * OWN, (t + 1) * OWN)
        inner = jnp.broadcast_to(s_all[t], (128, 128)).T[:OWN]
        sb = scale_b[rows, :]
        coef = (sb * sb * inner / D)[:, :1]
        gt_ref[rows, :] = (gs[rows, :] - x_ref[rows, :].astype(F32) * coef).astype(BF16)
    g_last()
    for j in range(NJ):
        step_d(j)

    def left(ref, s):
        copy(ref, ref, s, s, partner).wait_send()

    left(sq_all.at[pl.ds(0, NT - 1)], sq_s)
    left(s_all.at[pl.ds(0, NT - 1)], st_s)
    for h in range(NH):
        part = pl.ds(h * HW, HW)
        left(w_all.at[0, pl.ds(0, 9), :, :, part], wz_s.at[h])
        left(w_all.at[0, pl.ds(0, 13), 0, :, part], wx_s.at[h])
        left(w_all.at[:, :, 0, :, part], sib_s.at[h])
    left(tb.at[0], core_s.at[0])
    left(tb.at[0], core_s.at[1])
    left(xs, xs_s)
    left(leaf, leaf_s)
    left(gsend.at[0, pl.ds(0, 7)], chain_s)
    first = sum(6 if m == "y" else 4 for m in SUM_FIRST)
    left(r1.at[:, pl.ds(0, first // NJ)], r1_s)
    second = sum(1 if m == "y" else 3 for m in SUM_FIRST)
    left(r1.at[:, pl.ds(0, second // NJ)], r2_s)
    third = sum(1 if m == "y" else 3 for m in SEND_LAST)
    left(r1.at[:, pl.ds(0, third // NJ)], a1_s)
    fourth = sum(6 if m == "y" else 4 for m in SEND_LAST)
    left(r1.at[:, pl.ds(0, fourth // NJ)], a2_s)


def hand_over(val_in, gw_in, gt_in, val_out, gw_out, gt_out, sem):
    copies = [pltpu.make_async_copy(gw_in, gw_out, sem.at[8])]
    for q in range(4):
        rows = pl.ds(q * 128, 128)
        copies.append(pltpu.make_async_copy(val_in.at[rows], val_out.at[rows], sem.at[q]))
        copies.append(pltpu.make_async_copy(gt_in.at[rows], gt_out.at[rows], sem.at[4 + q]))
    for c in copies:
        c.start()
    for c in copies:
        c.wait()


def on_device(tokens, gain, w_value, cotangent):
    vmem = pl.BlockSpec(memory_space=pltpu.VMEM)
    dma = pltpu.SemaphoreType.DMA
    hbm = pl.BlockSpec(memory_space=pl.ANY)
    scratch = [
        pltpu.VMEM((ROWS, FEAT), BF16),
        pltpu.VMEM((ROWS, KV), BF16),
        pltpu.VMEM((1, FEAT), F32),
        pltpu.VMEM((2, NZ, 2, 16, KV), BF16),
        pltpu.VMEM((ROWS, FEAT), BF16),
        pltpu.VMEM((ROWS, 128), F32),
        pltpu.VMEM((1, ROWS), F32),
        pltpu.VMEM((NT, 1, ROWS), F32),
        pltpu.VMEM((2, NY, OWN, KV), BF16),
        pltpu.VMEM((NJ, 2 * NY, OWN, CW), BF16),
        pltpu.VMEM((NJ, NY, OWN, CW), BF16),
        pltpu.VMEM((NJ, NY, OWN, CW), BF16),
        pltpu.VMEM((ROWS, FEAT), F32),
        pltpu.VMEM((1, 128), F32),
        pltpu.VMEM((NT, 1, 128), F32),
        pltpu.VMEM((2, NZ, 2, 16, KV), F32),
        pltpu.VMEM((2, NZ, 16, KV), BF16),
        pltpu.VMEM((2, NZ, 16, KV), BF16),
        pltpu.VMEM((NZ, 16, KV), F32),
        pltpu.VMEM((NZ, 16, KV), BF16),
        pltpu.VMEM((NZ, 16, KV), BF16),
        pltpu.VMEM((2, 9, 16, KV), BF16),
        pltpu.VMEM((2, 4, 16, KV), BF16),
        pltpu.VMEM((2, 4, 16, KV), BF16),
        dma((NH,)), dma((NH, 2, 9)),
        dma((NH,)), dma((NH, 2, 9)),
        dma((NH,)), dma((NH,)),
        dma, dma,
        dma, dma,
        dma, dma((NJ,)),
        dma, dma((NJ,)),
        dma, dma((NJ,)),
        dma, dma((NJ,)),
        dma((2,)), dma((2,)),
        dma, dma((NZ,)),
        dma, dma((2, 4)),
        dma, dma((2, 4)),
        dma((10,)),
    ]
    values, grad_weight, grad_tokens = pl.pallas_call(
        kernel,
        name="value_projection",
        out_shape=(
            pltpu.VMEM((2, NY, OWN, KV), BF16),
            pltpu.VMEM((16, KV), F32),
            pltpu.VMEM((ROWS, FEAT), BF16),
        ),
        in_specs=[hbm] * 4,
        out_specs=(vmem,) * 3,
        scratch_shapes=scratch,
        cost_estimate=pl.CostEstimate(
            flops=6 * ROWS * FEAT * KV, bytes_accessed=8 * 2**20, transcendentals=ROWS
        ),
        compiler_params=pltpu.CompilerParams(
            collective_id=0, has_side_effects=True, vmem_limit_bytes=56 * 2**20
        ),
    )(tokens, gain.reshape(1, FEAT), w_value, cotangent)
    return pl.pallas_call(
        hand_over,
        name="hand_over",
        out_shape=(
            jax.ShapeDtypeStruct((ROWS, KV), BF16),
            jax.ShapeDtypeStruct((16, KV), F32),
            jax.ShapeDtypeStruct((ROWS, FEAT), BF16),
        ),
        in_specs=[vmem] * 3,
        out_specs=(hbm,) * 3,
        scratch_shapes=[dma((9,))],
        compiler_params=pltpu.CompilerParams(vmem_limit_bytes=16 * 2**20),
    )(values.reshape(ROWS, KV), grad_weight, grad_tokens)


def solution(mesh):
    return jax.shard_map(
        on_device,
        mesh=mesh,
        in_specs=(P("blk", "tp"), P("tp"), P(("tp", "blk"), None), P("blk", None)),
        out_specs=(P("blk", None), P(("tp", "blk"), None), P("blk", "tp")),
        check_vma=False,
    )
```
